32 devices in a mesh: req: 8 (over z, x), tp: 4 (over y, core).
Axes of the slice: x: 2, y: 2, z: 4, core: 2. Of those that a mesh axis runs over, the one named last changes fastest.
Arguments:
- hidden: bfloat16 [2048, 2048], P('req'), may hold values from -10.5 to 10.5
- lengths: int32 [8], replicated, may hold values from 1 to 1024, 2048 in all
- dealing: int32 [8], replicated, may hold values from 0 to 7, each once
- norm_gain: bfloat16 [2048], replicated, may hold values from 0.5 to 1.5
- w_query: bfloat16 [2048, 2048], P(None, 'tp'), may hold values from -0.125 to 0.125
- w_key: bfloat16 [2048, 1024], P(None, 'tp'), may hold values from -0.125 to 0.125
- w_value: bfloat16 [2048, 1024], P(None, 'tp'), may hold values from -0.125 to 0.125
- query_gain: bfloat16 [128], replicated, may hold values from 0.5 to 8
- key_gain: bfloat16 [128], replicated, may hold values from 0.5 to 8
- w_out: bfloat16 [2048, 2048], P(None, 'tp'), may hold values from -0.125 to 0.125
Outputs:
- hidden_out: bfloat16 [2048, 2048], P('req', 'tp')
- kv_cache: bfloat16 [2, 8, 1024, 1024], P(None, 'req', None, 'tp')
The draws below stay inside these ranges and needn't reach their ends.
Inputs may be any that keep to these rules, and one draw needn't show every extreme that they name: The lengths sum to 2048; the largest is exactly 1024. A permutation: dealt slot j, on device j of req, holds prompt dealing[j].
All inputs are finite; a program needn't handle non-finite values.
Results may differ from the reference program's by a relative error of at most 0.012.
The reference program's roundings to bfloat16 on the way count: a program that leaves them out, or rounds other values in their place, can miss the bound.
Values may be sent and summed in bfloat16 or wider, within the bound.
A program may use at most 128 MiB of HBM per device.

```python
import math
import jax
import jax.numpy as jnp
import numpy as np
from jax import lax

D = 2048
QH = 16
KVH = 8
HD = 128
TOK_DEV = 256
PROMPTS = 8
TOKENS = 2048
SEQ = 1024
N_REQ = 8


def draw_hidden(key, part):
    noise_key = jax.random.fold_in(key, 101)
    return jnp.clip(jax.random.normal(noise_key, (TOKENS, D), jnp.float32), -4.0, 4.0).astype(jnp.bfloat16)


def draw_query_gain(key, part):
    gain_key = jax.random.fold_in(key, 201)
    return jax.random.uniform(gain_key, (HD,), jnp.float32, 0.5, 2.0).astype(jnp.bfloat16)


def draw_key_gain(key, part):
    gain_key = jax.random.fold_in(key, 202)
    return jax.random.uniform(gain_key, (HD,), jnp.float32, 0.5, 2.0).astype(jnp.bfloat16)


def levels(rng, extent, pieces, least, largest):
    factor_of = 1.0
    for position, blocks in pieces:
        steps = jax.random.uniform(jax.random.fold_in(jax.random.fold_in(rng, 6), position), (blocks,), jnp.float32, least / len(pieces), largest / len(pieces))
        factor_of = factor_of * jnp.repeat(jnp.exp(steps), extent[position] // blocks).reshape((-1,) + (1,) * (len(extent) - 1 - position))
    return factor_of


def profile(amount, total, bound, lean):
    weights = [(1 << 20) // math.isqrt(grade ** lean) + 1 for grade in range(2, amount + 1)]
    surplus, holding = total - bound - (amount - 1), [1] * (amount - 1)
    while surplus > 0:
        movable = [i for i in range(amount - 1) if holding[i] < bound]
        whole, budget = sum([weights[i] for i in movable]), surplus
        for i in movable:
            addition = min(bound - holding[i], max(1, budget * weights[i] // whole), surplus)
            holding[i] = holding[i] + addition
            surplus = surplus - addition
    return np.array([bound] + holding)


def ragged_sizes(own_key, count, total, bound, lean):
    if count == 2:
        one = jax.random.randint(own_key, (), max(1, total - bound), min(bound, total - 1) + 1)
        return jnp.stack([one, total - one])
    sizes = jnp.asarray(profile(count, total, bound, lean), jnp.int32)
    twos = (count - 1) // 2
    giver, taker = sizes[1:1 + 2 * twos:2], sizes[2:2 + 2 * twos:2]
    room = jnp.minimum(giver - 1, bound - taker)
    shifted = jax.random.randint(jax.random.fold_in(own_key, 1), (twos,), 0, 1 << 20) % (room + 1)
    sizes = sizes.at[1:1 + 2 * twos:2].set(giver - shifted).at[2:2 + 2 * twos:2].set(taker + shifted)
    return sizes[jax.random.permutation(jax.random.fold_in(own_key, 2), count)]


def scatter_about(stream_key, dims, width, most, shards=(), kind=jnp.bfloat16):
    values = jax.random.normal(stream_key, dims, jnp.float32) * width
    if len(shards) > 0:
        values = levels(stream_key, dims, shards, -0.22, 0.18) * values
    return jnp.clip(values, min=-most, max=most).astype(kind)


def setup_inputs(seed: int = 0) -> dict:
    key_list = jax.random.split(jax.random.key(seed), 11)
    hidden = draw_hidden(jax.random.fold_in(key_list[10], 71), 0)
    lengths = ragged_sizes(key_list[1], PROMPTS, TOKENS, SEQ, 1).astype(jnp.int32)
    dealing = jax.random.permutation(key_list[2], PROMPTS).astype(jnp.int32)
    norm_gain = jnp.clip(1.0 + 0.1 * jax.random.normal(key_list[3], (D,), jnp.float32), 0.5, 1.5).astype(jnp.bfloat16)
    w_query = scatter_about(key_list[4], (D, QH * HD), D ** -0.5, 0.125, ((1, 4),))
    w_key = scatter_about(key_list[5], (D, KVH * HD), D ** -0.5, 0.125, ((1, 4),))
    w_value = scatter_about(key_list[6], (D, KVH * HD), D ** -0.5, 0.125, ((1, 4),))
    query_gain = draw_query_gain(jax.random.fold_in(key_list[10], 71), 0)
    key_gain = draw_key_gain(jax.random.fold_in(key_list[10], 71), 0)
    w_out = scatter_about(key_list[9], (QH * HD, D), (QH * HD) ** -0.5, 0.125, ((1, 4),))
    return dict(hidden=hidden, lengths=lengths, dealing=dealing, norm_gain=norm_gain, w_query=w_query, w_key=w_key, w_value=w_value, query_gain=query_gain, key_gain=key_gain, w_out=w_out)


EPS = 1e-06
THETA = 1000000.0

def rms_rows(values, scale_gain):
    inv_rms = lax.rsqrt(lax.optimization_barrier(jnp.mean(values * values, axis=-1, keepdims=True)) + EPS)
    return values * inv_rms * scale_gain

def rotate(values, positions):
    features = values.shape[-1]
    half_width = features // 2
    frequency = THETA ** (-(jnp.arange(half_width).astype(jnp.float32) * 2.0) / features)
    angles = positions.astype(jnp.float32)[:, None] * frequency[None, :]
    cosine = jnp.cos(angles)[:, None, :]
    sine_part = jnp.sin(angles)[:, None, :]
    first_half = values[..., :half_width]
    second_half = values[..., half_width:]
    return jnp.concatenate([first_half * cosine - second_half * sine_part, second_half * cosine + first_half * sine_part], axis=-1)

def attend_slot(operands):
    query_slot, key_slot, value_slot, slot_length = operands
    group_size = QH // KVH
    queries = query_slot.reshape(SEQ, KVH, group_size, HD).astype(jnp.float32)
    keys_split = key_slot.reshape(SEQ, KVH, HD).astype(jnp.float32)
    values_split = value_slot.reshape(SEQ, KVH, HD).astype(jnp.float32)
    scores = jnp.einsum('qkgd,skd->kgqs', queries, keys_split) * HD ** (-0.5)
    offsets = jnp.arange(SEQ, dtype=jnp.int32)
    allowed = (offsets[None, :] <= offsets[:, None]) & (offsets[None, :] < slot_length)
    scores = jnp.where(allowed[None, None], scores, -jnp.inf)
    row_max = lax.optimization_barrier(jnp.max(scores, axis=-1, keepdims=True))
    weights = jnp.exp(scores - row_max)
    weights = (weights / lax.optimization_barrier(jnp.sum(weights, axis=-1, keepdims=True))).astype(jnp.bfloat16)
    mixture = jnp.einsum('kgqs,skd->qkgd', weights.astype(jnp.float32), values_split)
    return mixture.astype(jnp.bfloat16).reshape(SEQ, QH * HD)

def reference(hidden, lengths, dealing, norm_gain, w_query, w_key, w_value, query_gain, key_gain, w_out):
    prompt_ends = jnp.cumsum(lengths).astype(jnp.int32)
    starts = (prompt_ends - lengths).astype(jnp.int32)
    packed_ids = jnp.arange(TOKENS, dtype=jnp.int32)
    segment = lax.optimization_barrier(jnp.sum((packed_ids[:, None] >= prompt_ends[None, :]).astype(jnp.int32), axis=1)).astype(jnp.int32)
    positions = (packed_ids - starts[segment]).astype(jnp.int32)
    packed = hidden.reshape(N_REQ, TOK_DEV, D).transpose(1, 0, 2).reshape(TOKENS, D)
    normed = rms_rows(packed.astype(jnp.float32), norm_gain.astype(jnp.float32)).astype(jnp.bfloat16)
    query_rows = jnp.dot(normed, w_query, preferred_element_type=jnp.float32).reshape(TOKENS, QH, HD)
    key_rows = jnp.dot(normed, w_key, preferred_element_type=jnp.float32).reshape(TOKENS, KVH, HD)
    value_rows = jnp.dot(normed, w_value, preferred_element_type=jnp.float32).astype(jnp.bfloat16)
    query_rows = rotate(rms_rows(query_rows, query_gain.astype(jnp.float32)), positions).astype(jnp.bfloat16).reshape(TOKENS, QH * HD)
    key_rows = rotate(rms_rows(key_rows, key_gain.astype(jnp.float32)), positions).astype(jnp.bfloat16).reshape(TOKENS, KVH * HD)
    offsets = jnp.arange(SEQ, dtype=jnp.int32)
    slot_lengths = lengths[dealing].astype(jnp.int32)
    slot_starts = starts[dealing].astype(jnp.int32)
    is_valid = offsets[None, :] < slot_lengths[:, None]
    row_ids = jnp.where(is_valid, slot_starts[:, None] + offsets[None, :], 0).astype(jnp.int32)

    def pick(source_table):
        return jnp.where(is_valid[:, :, None], source_table[row_ids], jnp.zeros((), source_table.dtype))
    query_slots = pick(query_rows)
    key_slots = pick(key_rows)
    value_slots = pick(value_rows)
    mixture = lax.map(attend_slot, (query_slots, key_slots, value_slots, slot_lengths)).reshape(PROMPTS * SEQ, QH * HD)
    inverse = jnp.zeros((PROMPTS,), jnp.int32).at[dealing].set(jnp.arange(PROMPTS, dtype=jnp.int32))
    slot_rows = (inverse[segment] * SEQ + positions).astype(jnp.int32)
    attended_packed = mixture[slot_rows]
    attended = attended_packed.reshape(TOK_DEV, N_REQ, QH * HD).transpose(1, 0, 2).reshape(TOKENS, QH * HD)
    branch = lax.optimization_barrier(jnp.dot(attended, w_out, preferred_element_type=jnp.float32).astype(jnp.bfloat16))
    hidden_out = (hidden.astype(jnp.float32) + branch.astype(jnp.float32)).astype(jnp.bfloat16)
    kv_cache = jnp.stack([key_slots, value_slots])
    return (hidden_out, kv_cache)
```

```python
import functools

import jax
import jax.numpy as jnp
import numpy as np
from jax import lax
from jax.experimental import pallas as pl
from jax.experimental.pallas import tpu as pltpu
from jax.sharding import PartitionSpec as P

EPS = 1e-06
THETA = 1000000.0


def rms_rows(values, scale_gain):
    inv_rms = lax.rsqrt(jnp.mean(values * values, axis=-1, keepdims=True) + EPS)
    return values * inv_rms * scale_gain


def rotate(values, positions):
    features = values.shape[-1]
    half_width = features // 2
    frequency = THETA ** (-(jnp.arange(half_width).astype(jnp.float32) * 2.0) / features)
    angles = positions.astype(jnp.float32)[:, None] * frequency[None, :]
    cosine = jnp.cos(angles)[:, None, :]
    sine_part = jnp.sin(angles)[:, None, :]
    first_half = values[..., :half_width]
    second_half = values[..., half_width:]
    return jnp.concatenate(
        [
            first_half * cosine - second_half * sine_part,
            second_half * cosine + first_half * sine_part,
        ],
        axis=-1,
    )


def project(normed, w_query, w_key, w_value, query_gain, key_gain, positions):
    head_dim = query_gain.shape[0]
    row_count = normed.shape[0]
    query_rows = jnp.dot(normed, w_query, preferred_element_type=jnp.float32).reshape(
        row_count, -1, head_dim
    )
    key_rows = jnp.dot(normed, w_key, preferred_element_type=jnp.float32).reshape(
        row_count, -1, head_dim
    )
    value_rows = jnp.dot(normed, w_value, preferred_element_type=jnp.float32).astype(jnp.bfloat16)
    query_rows = rotate(rms_rows(query_rows, query_gain.astype(jnp.float32)), positions).astype(
        jnp.bfloat16
    )
    key_rows = rotate(rms_rows(key_rows, key_gain.astype(jnp.float32)), positions).astype(
        jnp.bfloat16
    )
    return (query_rows.reshape(row_count, -1), key_rows.reshape(row_count, -1), value_rows)


def attend(query_slot, key_slot, value_slot, prompt_length, head_dim):
    slot_len, query_width = query_slot.shape
    kv_heads = key_slot.shape[1] // head_dim
    group_size = query_width // head_dim // kv_heads
    queries = query_slot.reshape(slot_len, kv_heads, group_size, head_dim)
    keys_split = key_slot.reshape(slot_len, kv_heads, head_dim)
    values_split = value_slot.reshape(slot_len, kv_heads, head_dim)
    scores = jnp.einsum(
        "qkgd,skd->kgqs", queries, keys_split, preferred_element_type=jnp.float32
    ) * head_dim ** (-0.5)
    offsets = jnp.arange(slot_len, dtype=jnp.int32)
    allowed = (offsets[None, :] <= offsets[:, None]) & (offsets[None, :] < prompt_length)
    scores = jnp.where(allowed[None, None], scores, -jnp.inf)
    row_max = jnp.max(scores, axis=-1, keepdims=True)
    weights = jnp.exp(scores - row_max)
    weights = (weights / jnp.sum(weights, axis=-1, keepdims=True)).astype(jnp.bfloat16)
    mixture = jnp.einsum(
        "kgqs,skd->qkgd", weights, values_split, preferred_element_type=jnp.float32
    )
    return mixture.astype(jnp.bfloat16).reshape(slot_len, query_width)


def on_device_ops(
    hidden, lengths, dealing, norm_gain, w_query, w_key, w_value, query_gain, key_gain, w_out
):
    devices = lax.axis_size("req")
    home_index = lax.axis_index("req")
    slice_index = lax.axis_index("tp")
    tok_rows, features = hidden.shape
    head_dim = query_gain.shape[0]
    out_width = w_out.shape[1]
    slot_len = 4 * tok_rows
    capacity = slot_len // devices
    prompt_total = lengths.shape[0]
    prompt_ids = jnp.arange(prompt_total, dtype=jnp.int32)
    prompt_ends = jnp.sum(
        jnp.where(prompt_ids[:, None] <= prompt_ids[None, :], lengths[:, None], 0), axis=0
    )
    starts = prompt_ends - lengths
    packed_ids = jnp.arange(tok_rows, dtype=jnp.int32) * devices + home_index
    segment = jnp.sum((packed_ids[:, None] >= prompt_ends[None, :]).astype(jnp.int32), axis=1)
    seg_onehot = (segment[:, None] == prompt_ids[None, :]).astype(jnp.int32)
    positions = packed_ids - jnp.sum(seg_onehot * starts[None, :], axis=1)
    inverse = jnp.zeros((prompt_total,), jnp.int32).at[dealing].set(prompt_ids)
    deal_hot = (dealing[:, None] == prompt_ids[None, :]).astype(jnp.int32)
    dealt_starts = jnp.sum(deal_hot * starts[None, :], axis=1)
    dealt_lengths = jnp.sum(deal_hot * lengths[None, :], axis=1)
    first_offset = jnp.mod(home_index - dealt_starts, devices)
    ranks = jnp.arange(capacity, dtype=jnp.int32)
    slot_offset = first_offset[None, :] + ranks[:, None] * devices
    send_valid = slot_offset < dealt_lengths[None, :]
    send_rows = jnp.where(
        send_valid, (dealt_starts[None, :] + slot_offset - home_index) // devices, 0
    ).reshape(-1)
    my_start = lax.dynamic_index_in_dim(dealt_starts, home_index, 0, keepdims=False)
    my_length = lax.dynamic_index_in_dim(dealt_lengths, home_index, 0, keepdims=False)
    roll_shift = jnp.mod(my_start, devices)
    my_slots = jnp.sum(seg_onehot * inverse[None, :], axis=1)
    back_rows = positions // devices * devices + my_slots
    offsets = jnp.arange(slot_len, dtype=jnp.int32)
    gain_values = norm_gain.astype(jnp.float32)
    picked = jnp.take(hidden, send_rows, axis=0).reshape(capacity, devices, hidden.shape[1])
    arrived = lax.all_to_all(
        jnp.where(send_valid[:, :, None], picked, jnp.zeros((), hidden.dtype)),
        "req",
        split_axis=1,
        concat_axis=1,
        tiled=True,
    )
    slot_hidden = jnp.roll(arrived, -roll_shift, axis=1).reshape(slot_len, arrived.shape[2])
    normed = rms_rows(slot_hidden.astype(jnp.float32), gain_values).astype(jnp.bfloat16)
    query_slot, key_slot, value_slot = project(
        normed, w_query, w_key, w_value, query_gain, key_gain, offsets
    )
    mixture = attend(query_slot, key_slot, value_slot, my_length, head_dim)
    sendback = jnp.roll(mixture.reshape(capacity, devices, mixture.shape[1]), roll_shift, axis=1)
    returned = lax.all_to_all(sendback, "req", split_axis=1, concat_axis=1, tiled=True)
    attended = jnp.take(returned.reshape(capacity * devices, -1), back_rows, axis=0)
    kv_cache = jnp.stack([key_slot, value_slot])[:, None]
    summed = jnp.dot(
        lax.all_gather(attended, "tp", axis=1, tiled=True),
        w_out,
        preferred_element_type=jnp.float32,
    )
    branch = lax.optimization_barrier(summed.astype(jnp.bfloat16))
    residual = lax.dynamic_slice_in_dim(hidden, slice_index * out_width, out_width, 1)
    hidden_out = (residual.astype(jnp.float32) + branch.astype(jnp.float32)).astype(jnp.bfloat16)
    return (hidden_out, kv_cache)


STAGES = 4
F32 = jnp.float32
BF16 = jnp.bfloat16
MESH = pl.DeviceIdType.MESH


def flip(index, mask):
    flipped = index
    bit = 1
    while bit <= mask:
        if mask & bit:
            flipped = flipped + bit * (1 - 2 * ((index // bit) % 2))
        bit *= 2
    return flipped


def pick(which, choices):
    total = jnp.zeros_like(which)
    for place, choice in enumerate(choices):
        total = total + jnp.where(which == place, choice, 0)
    return total


def whole_kernel(
    n, len_ref, deal_ref, hid_ref, gain_ref, qg_ref, kg_ref, cos_ref, sin_ref,
    wq_hbm, wk_hbm, wv_hbm, wo_hbm, out_ref, kv_ref,
    wq, wk, wv, wo, snd, arr, xs, sb, ret, att,
    w_sem, d_send, d_recv, f_send, f_recv, r_send, r_recv, a_send, a_recv,
):
    me = lax.axis_index("req")
    t = lax.axis_index("tp")
    yp = flip(t, 2)
    sib = flip(t, 1)
    tok = hid_ref.shape[0]
    width = wq.shape[1]
    head = qg_ref.shape[1]
    q_heads = width // head
    kv_heads = wk.shape[1] // head
    group = q_heads // kv_heads
    part = xs.shape[3]
    parts = xs.shape[1]
    run = arr.shape[2]
    block = n * run

    weight_copies = [
        pltpu.make_async_copy(source, target, w_sem.at[k])
        for k, (source, target) in enumerate(
            ((wq_hbm, wq), (wk_hbm, wk), (wv_hbm, wv), (wo_hbm, wo))
        )
    ]
    for copy in weight_copies:
        copy.start()

    barrier = pltpu.get_barrier_semaphore()
    for o in range(1, n):
        pl.semaphore_signal(barrier, inc=1, device_id={"req": flip(me, o)}, device_id_type=MESH)
    for peer in (yp, sib):
        pl.semaphore_signal(barrier, inc=1, device_id={"tp": peer}, device_id_type=MESH)

    prompts = len_ref.shape[0]
    lens = [len_ref[p] for p in range(prompts)]
    starts = [jnp.int32(0)]
    for p in range(prompts - 1):
        starts.append(starts[-1] + lens[p])
    dealt = [deal_ref[j] for j in range(n)]
    d_start = [pick(d, starts) for d in dealt]
    d_len = [pick(d, lens) for d in dealt]
    first = [lax.rem(me - s + n * tok, n) for s in d_start]
    base = [lax.div(s + f - me, n) for s, f in zip(d_start, first)]
    my_start = pick(me, d_start)
    my_len = pick(me, d_len)

    def chosen(index, stage, rows):
        source = index // run
        step = index % run + stage * run
        return (rows == pick(source, base) + step) & (
            pick(source, first) + n * step < pick(source, d_len)
        )

    col = lax.broadcasted_iota(jnp.int32, (block, 1), 0)
    row = lax.broadcasted_iota(jnp.int32, (1, block), 1)
    tok_row = lax.broadcasted_iota(jnp.int32, (1, tok), 1)
    tok_col = lax.broadcasted_iota(jnp.int32, (tok, 1), 0)

    def place(index):
        return n * (index % run) + lax.rem(index // run - my_start + n * tok, n)

    to_slot = jnp.where(col == place(row), 1.0, 0.0).astype(BF16)
    to_source = jnp.where(place(col) == row, 1.0, 0.0).astype(BF16)

    own = pl.ds(pl.multiple_of(t * part, part), part)
    hid = hid_ref[...].astype(F32)
    inv = lax.rsqrt(jnp.mean(hid * hid, axis=-1, keepdims=True) + EPS)
    normed = (hid_ref[:, own].astype(F32) * inv * gain_ref[:, own].astype(F32)).astype(BF16)

    def dispatch(i, o):
        peer = flip(me, o)
        return pltpu.make_async_remote_copy(
            src_ref=snd.at[i, peer], dst_ref=arr.at[i, me],
            send_sem=d_send.at[i, o], recv_sem=d_recv.at[i, o],
            device_id={"req": peer}, device_id_type=MESH,
        )

    def giveback(i, o):
        peer = flip(me, o)
        return pltpu.make_async_remote_copy(
            src_ref=sb.at[i, peer], dst_ref=ret.at[i, me],
            send_sem=r_send.at[i, o], recv_sem=r_recv.at[i, o],
            device_id={"req": peer}, device_id_type=MESH,
        )

    def spread(i, k):
        which = yp if k == 2 else t
        return pltpu.make_async_remote_copy(
            src_ref=xs.at[i, which], dst_ref=xs.at[i, which],
            send_sem=f_send.at[i, k], recv_sem=f_recv.at[i, k],
            device_id={"tp": yp if k == 0 else sib}, device_id_type=MESH,
        )

    def share(k):
        which = yp if k == 2 else t
        return pltpu.make_async_remote_copy(
            src_ref=att.at[which], dst_ref=att.at[which],
            send_sem=a_send.at[k], recv_sem=a_recv.at[k],
            device_id={"tp": yp if k == 0 else sib}, device_id_type=MESH,
        )

    order = sorted(range(1, n), key=lambda o: (-(o // 2), o))
    for i in range(STAGES):
        select = jnp.where(chosen(col, i, tok_row), 1.0, 0.0).astype(BF16)
        rows = jnp.dot(select, normed, preferred_element_type=F32).astype(BF16)
        snd[i] = rows.reshape(n, run, part)
        if i == 0:
            pl.semaphore_wait(barrier, n + 1)
        for o in order:
            dispatch(i, o).start()

    def first_hop(i):
        arr[i, me] = snd[i, me]
        for o in order:
            dispatch(i, o).wait_recv()
        xs[i, t] = jnp.dot(
            to_slot, arr[i].reshape(block, part), preferred_element_type=F32
        ).astype(BF16)
        spread(i, 0).start()
        spread(i, 1).start()

    def second_hop(i):
        spread(i, 0).wait_recv()
        spread(i, 2).start()

    def turn(values, gain, i):
        rows = slice(i * block, (i + 1) * block)
        scaled = values * lax.rsqrt(jnp.mean(values * values, axis=-1, keepdims=True) + EPS)
        scaled = scaled * gain
        swapped = pltpu.roll(scaled, head // 2, 1)
        return (scaled * cos_ref[rows, :] + swapped * sin_ref[rows, :]).astype(BF16)

    def project_stage(weights, i):
        total = jnp.dot(xs[i, 0], weights[:part, :], preferred_element_type=F32)
        for q in range(1, parts):
            total += jnp.dot(
                xs[i, q], weights[q * part : (q + 1) * part, :], preferred_element_type=F32
            )
        return total

    def compute(i):
        spread(i, 1).wait_recv()
        spread(i, 2).wait_recv()
        rows = slice(i * block, (i + 1) * block)
        extent = (i + 1) * block
        query_gain = qg_ref[...].astype(F32)
        key_gain = kg_ref[...].astype(F32)
        query = project_stage(wq, i)
        key = project_stage(wk, i)
        kv_ref[1, 0, rows, :] = project_stage(wv, i).astype(BF16)
        for g in range(kv_heads):
            lanes = slice(g * head, (g + 1) * head)
            kv_ref[0, 0, rows, lanes] = turn(key[:, lanes], key_gain, i)
        q_pos = lax.broadcasted_iota(jnp.int32, (block, extent), 0) + i * block
        k_pos = lax.broadcasted_iota(jnp.int32, (block, extent), 1)
        allowed = (k_pos <= q_pos) & (k_pos < my_len)
        mixed = []
        for h in range(q_heads):
            lanes = slice(h // group * head, (h // group + 1) * head)
            turned = turn(query[:, h * head : (h + 1) * head], query_gain, i)
            scores = lax.dot_general(
                turned, kv_ref[0, 0, :extent, lanes], (((1,), (1,)), ((), ())),
                preferred_element_type=F32,
            ) * head ** (-0.5)
            scores = jnp.where(allowed, scores, -jnp.inf)
            weights = jnp.exp(scores - jnp.max(scores, axis=-1, keepdims=True))
            weights = weights * (1.0 / jnp.sum(weights, axis=-1, keepdims=True))
            mixed.append(
                jnp.dot(
                    weights.astype(BF16), kv_ref[1, 0, :extent, lanes],
                    preferred_element_type=F32,
                ).astype(BF16)
            )
        back = jnp.dot(to_source, jnp.concatenate(mixed, axis=1), preferred_element_type=F32)
        sb[i] = back.astype(BF16).reshape(n, run, width)
        for o in order:
            giveback(i, o).start()
        ret[i, me] = sb[i, me]

    first_hop(0)
    second_hop(0)
    for copy in weight_copies:
        copy.wait()
    for i in range(STAGES):
        if i + 1 < STAGES:
            first_hop(i + 1)
        compute(i)
        if i + 1 < STAGES:
            second_hop(i + 1)

    total = jnp.zeros((tok, width), F32)
    for i in range(STAGES):
        for o in order:
            giveback(i, o).wait_recv()
        select = jnp.where(chosen(row, i, tok_col), 1.0, 0.0).astype(BF16)
        total += jnp.dot(select, ret[i].reshape(block, width), preferred_element_type=F32)
    att[t] = total.astype(BF16)
    share(0).start()
    share(1).start()
    share(0).wait_recv()
    share(2).start()
    share(1).wait_recv()
    share(2).wait_recv()
    summed = jnp.dot(att[0], wo[:width, :], preferred_element_type=F32)
    for q in range(1, parts):
        summed += jnp.dot(
            att[q], wo[q * width : (q + 1) * width, :], preferred_element_type=F32
        )
    branch = summed.astype(BF16).astype(F32)
    out_ref[...] = (hid_ref[:, own].astype(F32) + branch).astype(BF16)

    for i in range(STAGES):
        for o in order:
            dispatch(i, o).wait_send()
            giveback(i, o).wait_send()
        for k in range(3):
            spread(i, k).wait_send()
    for k in range(3):
        share(k).wait_send()


def on_device(
    hidden, lengths, dealing, norm_gain, w_query, w_key, w_value, query_gain, key_gain, w_out
):
    n = lax.axis_size("req")
    parts = lax.axis_size("tp")
    tok, features = hidden.shape
    head = query_gain.shape[0]
    width = w_query.shape[1]
    kv_width = w_key.shape[1]
    out_width = w_out.shape[1]
    slot_len = 4 * tok
    run = slot_len // n // STAGES
    if n != 8 or parts != 4 or run % 16:
        return on_device_ops(
            hidden, lengths, dealing, norm_gain, w_query, w_key, w_value, query_gain, key_gain, w_out
        )
    half = head // 2
    frequency = (THETA ** (-(np.arange(half) * 2.0) / head)).astype(np.float32)
    angles = np.arange(slot_len, dtype=np.float32)[:, None] * frequency[None, :]
    cosine = np.cos(angles.astype(np.float64)).astype(np.float32)
    sine = np.sin(angles.astype(np.float64)).astype(np.float32)
    cosines = jnp.asarray(np.concatenate([cosine, cosine], axis=1))
    sines = jnp.asarray(np.concatenate([-sine, sine], axis=1))
    part = features // parts
    smem = pl.BlockSpec(memory_space=pltpu.SMEM)
    vmem = pl.BlockSpec(memory_space=pltpu.VMEM)
    hbm = pl.BlockSpec(memory_space=pl.ANY)
    dma = pltpu.SemaphoreType.DMA
    hidden_out, kv_cache = pl.pallas_call(
        functools.partial(whole_kernel, n),
        out_shape=(
            jax.ShapeDtypeStruct((tok, out_width), BF16),
            jax.ShapeDtypeStruct((2, 1, slot_len, kv_width), BF16),
        ),
        in_specs=[smem] * 2 + [vmem] * 6 + [hbm] * 4,
        out_specs=(vmem, vmem),
        scratch_shapes=[
            pltpu.VMEM(w_query.shape, BF16),
            pltpu.VMEM(w_key.shape, BF16),
            pltpu.VMEM(w_value.shape, BF16),
            pltpu.VMEM(w_out.shape, BF16),
            pltpu.VMEM((STAGES, n, run, part), BF16),
            pltpu.VMEM((STAGES, n, run, part), BF16),
            pltpu.VMEM((STAGES, parts, n * run, part), BF16),
            pltpu.VMEM((STAGES, n, run, width), BF16),
            pltpu.VMEM((STAGES, n, run, width), BF16),
            pltpu.VMEM((parts, tok, width), BF16),
            dma((4,)),
            dma((STAGES, n)),
            dma((STAGES, n)),
            dma((STAGES, 3)),
            dma((STAGES, 3)),
            dma((STAGES, n)),
            dma((STAGES, n)),
            dma((3,)),
            dma((3,)),
        ],
        compiler_params=pltpu.CompilerParams(
            collective_id=0, has_side_effects=True, vmem_limit_bytes=56 * 2**20
        ),
        name="attention_half",
    )(
        lengths, dealing, hidden, norm_gain.reshape(1, -1), query_gain.reshape(1, -1),
        key_gain.reshape(1, -1), cosines, sines, w_query, w_key, w_value, w_out,
    )
    return hidden_out, kv_cache


def solution(mesh):
    in_specs = (
        P("req", None),
        P(),
        P(),
        P(),
        P(None, "tp"),
        P(None, "tp"),
        P(None, "tp"),
        P(),
        P(),
        P(None, "tp"),
    )
    out_specs = (P("req", "tp"), P(None, "req", None, "tp"))
    return jax.shard_map(
        on_device, mesh=mesh, in_specs=in_specs, out_specs=out_specs, check_vma=False
    )
```

```python
import functools

import jax
import jax.numpy as jnp
import numpy as np
from jax import lax
from jax.experimental import pallas as pl
from jax.experimental.pallas import tpu as pltpu
from jax.sharding import PartitionSpec as P

EPS = 1e-06
THETA = 1000000.0


def rms_rows(values, scale_gain):
    inv_rms = lax.rsqrt(jnp.mean(values * values, axis=-1, keepdims=True) + EPS)
    return values * inv_rms * scale_gain


def rotate(values, positions):
    features = values.shape[-1]
    half_width = features // 2
    frequency = THETA ** (-(jnp.arange(half_width).astype(jnp.float32) * 2.0) / features)
    angles = positions.astype(jnp.float32)[:, None] * frequency[None, :]
    cosine = jnp.cos(angles)[:, None, :]
    sine_part = jnp.sin(angles)[:, None, :]
    first_half = values[..., :half_width]
    second_half = values[..., half_width:]
    return jnp.concatenate(
        [
            first_half * cosine - second_half * sine_part,
            second_half * cosine + first_half * sine_part,
        ],
        axis=-1,
    )


def project(normed, w_query, w_key, w_value, query_gain, key_gain, positions):
    head_dim = query_gain.shape[0]
    row_count = normed.shape[0]
    query_rows = jnp.dot(normed, w_query, preferred_element_type=jnp.float32).reshape(
        row_count, -1, head_dim
    )
    key_rows = jnp.dot(normed, w_key, preferred_element_type=jnp.float32).reshape(
        row_count, -1, head_dim
    )
    value_rows = jnp.dot(normed, w_value, preferred_element_type=jnp.float32).astype(jnp.bfloat16)
    query_rows = rotate(rms_rows(query_rows, query_gain.astype(jnp.float32)), positions).astype(
        jnp.bfloat16
    )
    key_rows = rotate(rms_rows(key_rows, key_gain.astype(jnp.float32)), positions).astype(
        jnp.bfloat16
    )
    return (query_rows.reshape(row_count, -1), key_rows.reshape(row_count, -1), value_rows)


def attend(query_slot, key_slot, value_slot, prompt_length, head_dim):
    slot_len, query_width = query_slot.shape
    kv_heads = key_slot.shape[1] // head_dim
    group_size = query_width // head_dim // kv_heads
    queries = query_slot.reshape(slot_len, kv_heads, group_size, head_dim)
    keys_split = key_slot.reshape(slot_len, kv_heads, head_dim)
    values_split = value_slot.reshape(slot_len, kv_heads, head_dim)
    scores = jnp.einsum(
        "qkgd,skd->kgqs", queries, keys_split, preferred_element_type=jnp.float32
    ) * head_dim ** (-0.5)
    offsets = jnp.arange(slot_len, dtype=jnp.int32)
    allowed = (offsets[None, :] <= offsets[:, None]) & (offsets[None, :] < prompt_length)
    scores = jnp.where(allowed[None, None], scores, -jnp.inf)
    row_max = jnp.max(scores, axis=-1, keepdims=True)
    weights = jnp.exp(scores - row_max)
    weights = (weights / jnp.sum(weights, axis=-1, keepdims=True)).astype(jnp.bfloat16)
    mixture = jnp.einsum(
        "kgqs,skd->qkgd", weights, values_split, preferred_element_type=jnp.float32
    )
    return mixture.astype(jnp.bfloat16).reshape(slot_len, query_width)


def on_device_ops(
    hidden, lengths, dealing, norm_gain, w_query, w_key, w_value, query_gain, key_gain, w_out
):
    devices = lax.axis_size("req")
    home_index = lax.axis_index("req")
    slice_index = lax.axis_index("tp")
    tok_rows, features = hidden.shape
    head_dim = query_gain.shape[0]
    out_width = w_out.shape[1]
    slot_len = 4 * tok_rows
    capacity = slot_len // devices
    prompt_total = lengths.shape[0]
    prompt_ids = jnp.arange(prompt_total, dtype=jnp.int32)
    prompt_ends = jnp.sum(
        jnp.where(prompt_ids[:, None] <= prompt_ids[None, :], lengths[:, None], 0), axis=0
    )
    starts = prompt_ends - lengths
    packed_ids = jnp.arange(tok_rows, dtype=jnp.int32) * devices + home_index
    segment = jnp.sum((packed_ids[:, None] >= prompt_ends[None, :]).astype(jnp.int32), axis=1)
    seg_onehot = (segment[:, None] == prompt_ids[None, :]).astype(jnp.int32)
    positions = packed_ids - jnp.sum(seg_onehot * starts[None, :], axis=1)
    inverse = jnp.zeros((prompt_total,), jnp.int32).at[dealing].set(prompt_ids)
    deal_hot = (dealing[:, None] == prompt_ids[None, :]).astype(jnp.int32)
    dealt_starts = jnp.sum(deal_hot * starts[None, :], axis=1)
    dealt_lengths = jnp.sum(deal_hot * lengths[None, :], axis=1)
    first_offset = jnp.mod(home_index - dealt_starts, devices)
    ranks = jnp.arange(capacity, dtype=jnp.int32)
    slot_offset = first_offset[None, :] + ranks[:, None] * devices
    send_valid = slot_offset < dealt_lengths[None, :]
    send_rows = jnp.where(
        send_valid, (dealt_starts[None, :] + slot_offset - home_index) // devices, 0
    ).reshape(-1)
    my_start = lax.dynamic_index_in_dim(dealt_starts, home_index, 0, keepdims=False)
    my_length = lax.dynamic_index_in_dim(dealt_lengths, home_index, 0, keepdims=False)
    roll_shift = jnp.mod(my_start, devices)
    my_slots = jnp.sum(seg_onehot * inverse[None, :], axis=1)
    back_rows = positions // devices * devices + my_slots
    offsets = jnp.arange(slot_len, dtype=jnp.int32)
    gain_values = norm_gain.astype(jnp.float32)
    picked = jnp.take(hidden, send_rows, axis=0).reshape(capacity, devices, hidden.shape[1])
    arrived = lax.all_to_all(
        jnp.where(send_valid[:, :, None], picked, jnp.zeros((), hidden.dtype)),
        "req",
        split_axis=1,
        concat_axis=1,
        tiled=True,
    )
    slot_hidden = jnp.roll(arrived, -roll_shift, axis=1).reshape(slot_len, arrived.shape[2])
    normed = rms_rows(slot_hidden.astype(jnp.float32), gain_values).astype(jnp.bfloat16)
    query_slot, key_slot, value_slot = project(
        normed, w_query, w_key, w_value, query_gain, key_gain, offsets
    )
    mixture = attend(query_slot, key_slot, value_slot, my_length, head_dim)
    sendback = jnp.roll(mixture.reshape(capacity, devices, mixture.shape[1]), roll_shift, axis=1)
    returned = lax.all_to_all(sendback, "req", split_axis=1, concat_axis=1, tiled=True)
    attended = jnp.take(returned.reshape(capacity * devices, -1), back_rows, axis=0)
    kv_cache = jnp.stack([key_slot, value_slot])[:, None]
    summed = jnp.dot(
        lax.all_gather(attended, "tp", axis=1, tiled=True),
        w_out,
        preferred_element_type=jnp.float32,
    )
    branch = lax.optimization_barrier(summed.astype(jnp.bfloat16))
    residual = lax.dynamic_slice_in_dim(hidden, slice_index * out_width, out_width, 1)
    hidden_out = (residual.astype(jnp.float32) + branch.astype(jnp.float32)).astype(jnp.bfloat16)
    return (hidden_out, kv_cache)


STAGES = 4
F32 = jnp.float32
BF16 = jnp.bfloat16
MESH = pl.DeviceIdType.MESH


def flip(index, mask):
    flipped = index
    bit = 1
    while bit <= mask:
        if mask & bit:
            flipped = flipped + bit * (1 - 2 * ((index // bit) % 2))
        bit *= 2
    return flipped


def pick(which, choices):
    total = jnp.zeros_like(which)
    for place, choice in enumerate(choices):
        total = total + jnp.where(which == place, choice, 0)
    return total


def whole_kernel(
    n, len_ref, deal_ref, hid_ref, gain_ref, qg_ref, kg_ref, table_ref,
    wq_hbm, wk_hbm, wv_hbm, wo_hbm, out_ref, kv_ref,
    wq, wk, wv, wo, kvb, scores, picked, att,
    w_sem, m_send, m_recv, a_send, a_recv,
):
    me = lax.axis_index("req")
    t = lax.axis_index("tp")
    yp = flip(t, 2)
    sib = flip(t, 1)
    tok = hid_ref.shape[0]
    width = wq.shape[1]
    kv_width = wk.shape[1]
    head = qg_ref.shape[1]
    kv_heads = kv_width // head
    group = width // head // kv_heads
    out_width = out_ref.shape[1]
    parts = att.shape[0]
    piece = group * head
    half = tok // 2
    slot_len = table_ref.shape[0]
    run = picked.shape[2]
    block = n * run

    weight_copies = [
        pltpu.make_async_copy(source, target, w_sem.at[k])
        for k, (source, target) in enumerate(
            ((wk_hbm, wk), (wv_hbm, wv), (wq_hbm, wq), (wo_hbm, wo))
        )
    ]
    for copy in weight_copies:
        copy.start()

    barrier = pltpu.get_barrier_semaphore()
    far = (4, 6, 2)
    for o in (1,) + far:
        pl.semaphore_signal(barrier, inc=1, device_id={"req": flip(me, o)}, device_id_type=MESH)
    for peer in (yp, sib):
        pl.semaphore_signal(barrier, inc=1, device_id={"tp": peer}, device_id_type=MESH)

    prompts = len_ref.shape[0]
    lens = [len_ref[p] for p in range(prompts)]
    starts = [jnp.int32(0)]
    for p in range(prompts - 1):
        starts.append(starts[-1] + lens[p])
    mine = pick(me, [deal_ref[j] for j in range(n)])
    my_start = pick(mine, starts)
    my_len = pick(mine, lens)

    row = lax.broadcasted_iota(jnp.int32, (1, tok), 1)
    col = lax.broadcasted_iota(jnp.int32, (tok, 1), 0)
    token = col * n + me
    token_start = jnp.zeros_like(token)
    for start in starts[1:]:
        token_start = jnp.maximum(token_start, jnp.where(token >= start, start, 0))

    slots = lax.broadcasted_iota(jnp.int32, (1, slot_len), 1)
    at_position = jnp.where(token - token_start == slots, 1.0, 0.0).astype(BF16)
    terms = jnp.dot(at_position, table_ref[...], preferred_element_type=F32)
    turns = terms[:, : 2 * head] + terms[:, 2 * head : 4 * head] + terms[:, 4 * head :]
    cosines, sines = turns[:, :head], turns[:, head:]

    hid = hid_ref[...].astype(F32)
    inv = lax.rsqrt(jnp.mean(hid * hid, axis=-1, keepdims=True) + EPS)
    normed = (hid * inv * gain_ref[...].astype(F32)).astype(BF16)

    def turn(values, gain):
        scaled = values * lax.rsqrt(jnp.mean(values * values, axis=-1, keepdims=True) + EPS)
        scaled = scaled * gain
        return (scaled * cosines + pltpu.roll(scaled, head // 2, 1) * sines).astype(BF16)

    def move(o, h, onward):
        source = flip(me, o) if onward else me
        rows = pl.ds(h * half, half)
        slot = o + 1 if onward else o
        return pltpu.make_async_remote_copy(
            src_ref=kvb.at[source, rows], dst_ref=kvb.at[source, rows],
            send_sem=m_send.at[slot, h], recv_sem=m_recv.at[slot, h],
            device_id={"req": flip(me, 1 if onward else o)}, device_id_type=MESH,
        )

    def share(k, g):
        which = yp if k == 2 else t
        return pltpu.make_async_remote_copy(
            src_ref=att.at[which, g], dst_ref=att.at[which, g],
            send_sem=a_send.at[k, g], recv_sem=a_recv.at[k, g],
            device_id={"tp": yp if k == 0 else sib}, device_id_type=MESH,
        )

    weight_copies[0].wait()
    weight_copies[1].wait()
    key = jnp.dot(normed, wk[...], preferred_element_type=F32)
    value = jnp.dot(normed, wv[...], preferred_element_type=F32)
    key_gain = kg_ref[...].astype(F32)
    for g in range(kv_heads):
        lanes = slice(g * head, (g + 1) * head)
        kvb[me, :, lanes] = turn(key[:, lanes], key_gain)
    kvb[me, :, kv_width:] = value.astype(BF16)
    pl.semaphore_wait(barrier, 6)
    for h in range(2):
        for o in far:
            move(o, h, False).start()
        move(0, h, True).start()

    weight_copies[2].wait()
    query = jnp.dot(normed, wq[...], preferred_element_type=F32)
    query_gain = qg_ref[...].astype(F32)
    queries = [
        turn(query[:, h * head : (h + 1) * head], query_gain) for h in range(width // head)
    ]

    def onward(o, h):
        move(o, h, False).wait_recv()
        move(o, h, True).start()

    def wait_for(o):
        for h in range(2):
            move(o - 1, h, True).wait_recv()

    def meet(o):
        source = flip(me, o)
        key_token = row * n + source
        allowed = (key_token <= token) & (key_token >= token_start)
        for h in range(width // head):
            g = h // group
            product = lax.dot_general(
                queries[h], kvb[source, :, g * head : (g + 1) * head],
                (((1,), (1,)), ((), ())), preferred_element_type=F32,
            )
            scores[h, :, o * tok : (o + 1) * tok] = jnp.where(
                allowed, product * head ** (-0.5), -jnp.inf
            )
        first = lax.rem(source - my_start + n * tok, n)
        begin = lax.div(my_start + first - source, n)
        step = lax.broadcasted_iota(jnp.int32, (slot_len // n, 1), 0)
        select = (row == begin + step) & (first + n * step < my_len)
        rows = jnp.dot(
            jnp.where(select, 1.0, 0.0).astype(BF16), kvb[source], preferred_element_type=F32
        ).astype(BF16)
        for i in range(STAGES):
            picked[i, source] = rows[i * run : (i + 1) * run]

    onward(2, 0)
    onward(2, 1)
    meet(0)
    onward(4, 0)
    onward(6, 0)
    wait_for(1)
    meet(1)
    meet(2)
    onward(4, 1)
    onward(6, 1)
    meet(4)
    meet(6)
    for o in (3, 5, 7):
        wait_for(o)
        meet(o)

    for g in range(kv_heads):
        for k in range(group):
            h = g * group + k
            whole = scores[h]
            weights = jnp.exp(whole - jnp.max(whole, axis=-1, keepdims=True))
            weights = weights * (1.0 / jnp.sum(weights, axis=-1, keepdims=True))
            weights = weights.astype(BF16)
            lanes = slice(kv_width + g * head, kv_width + (g + 1) * head)
            mixed = jnp.zeros((tok, head), F32)
            for o in range(n):
                mixed += jnp.dot(
                    weights[:, o * tok : (o + 1) * tok], kvb[flip(me, o), :, lanes],
                    preferred_element_type=F32,
                )
            att[t, g, :, k * head : (k + 1) * head] = mixed.astype(BF16)
        share(0, g).start()
        share(1, g).start()

    share(0, 0).wait_recv()
    share(2, 0).start()

    place = n * (row % run) + lax.rem(row // run - my_start + n * tok, n)
    to_slot = jnp.where(col == place, 1.0, 0.0).astype(BF16)
    for i in range(STAGES):
        rows = jnp.dot(
            to_slot, picked[i].reshape(block, 2 * kv_width), preferred_element_type=F32
        ).astype(BF16)
        kv_ref[0, 0, i * block : (i + 1) * block, :] = rows[:, :kv_width]
        kv_ref[1, 0, i * block : (i + 1) * block, :] = rows[:, kv_width:]

    share(0, 1).wait_recv()
    share(2, 1).start()
    weight_copies[3].wait()
    for g in range(kv_heads):
        share(1, g).wait_recv()
        share(2, g).wait_recv()
    summed = jnp.zeros((tok, out_width), F32)
    for q in range(parts):
        for g in range(kv_heads):
            begin = q * width + g * piece
            summed += jnp.dot(att[q, g], wo[begin : begin + piece, :], preferred_element_type=F32)
    own = pl.ds(pl.multiple_of(t * out_width, out_width), out_width)
    branch = summed.astype(BF16).astype(F32)
    out_ref[...] = (hid_ref[:, own].astype(F32) + branch).astype(BF16)

    for h in range(2):
        for o in far:
            move(o, h, False).wait_send()
        for o in (0, 2, 4, 6):
            move(o, h, True).wait_send()
    for g in range(kv_heads):
        for k in range(3):
            share(k, g).wait_send()


def on_device(
    hidden, lengths, dealing, norm_gain, w_query, w_key, w_value, query_gain, key_gain, w_out
):
    n = lax.axis_size("req")
    parts = lax.axis_size("tp")
    tok, features = hidden.shape
    head = query_gain.shape[0]
    width = w_query.shape[1]
    kv_width = w_key.shape[1]
    out_width = w_out.shape[1]
    slot_len = 4 * tok
    run = slot_len // n // STAGES
    if n != 8 or parts != 4 or run % 16 or n * run != tok:
        return on_device_ops(
            hidden, lengths, dealing, norm_gain, w_query, w_key, w_value, query_gain, key_gain, w_out
        )
    half = head // 2
    frequency = (THETA ** (-(np.arange(half) * 2.0) / head)).astype(np.float32)
    angles = np.arange(slot_len, dtype=np.float32)[:, None] * frequency[None, :]
    cosine = np.cos(angles.astype(np.float64)).astype(np.float32)
    sine = np.sin(angles.astype(np.float64)).astype(np.float32)
    exact = np.concatenate([cosine, cosine, -sine, sine], axis=1)
    terms = []
    for _ in range(3):
        terms.append(exact.astype(jnp.bfloat16))
        exact = exact - terms[-1].astype(np.float32)
    table = jnp.asarray(np.concatenate(terms, axis=1))
    smem = pl.BlockSpec(memory_space=pltpu.SMEM)
    vmem = pl.BlockSpec(memory_space=pltpu.VMEM)
    hbm = pl.BlockSpec(memory_space=pl.ANY)
    dma = pltpu.SemaphoreType.DMA
    hidden_out, kv_cache = pl.pallas_call(
        functools.partial(whole_kernel, n),
        out_shape=(
            jax.ShapeDtypeStruct((tok, out_width), BF16),
            jax.ShapeDtypeStruct((2, 1, slot_len, kv_width), BF16),
        ),
        in_specs=[smem] * 2 + [vmem] * 5 + [hbm] * 4,
        out_specs=(vmem, vmem),
        scratch_shapes=[
            pltpu.VMEM(w_query.shape, BF16),
            pltpu.VMEM(w_key.shape, BF16),
            pltpu.VMEM(w_value.shape, BF16),
            pltpu.VMEM(w_out.shape, BF16),
            pltpu.VMEM((n, tok, 2 * kv_width), BF16),
            pltpu.VMEM((width // head, tok, n * tok), F32),
            pltpu.VMEM((STAGES, n, run, 2 * kv_width), BF16),
            pltpu.VMEM((parts, kv_width // head, tok, width * head // kv_width), BF16),
            dma((4,)),
            dma((n, 2)),
            dma((n, 2)),
            dma((3, kv_width // head)),
            dma((3, kv_width // head)),
        ],
        compiler_params=pltpu.CompilerParams(
            collective_id=0, has_side_effects=True, vmem_limit_bytes=56 * 2**20
        ),
        name="attention_half",
    )(
        lengths, dealing, hidden, norm_gain.reshape(1, -1), query_gain.reshape(1, -1),
        key_gain.reshape(1, -1), table, w_query, w_key, w_value, w_out,
    )
    return hidden_out, kv_cache


def solution(mesh):
    in_specs = (
        P("req", None),
        P(),
        P(),
        P(),
        P(None, "tp"),
        P(None, "tp"),
        P(None, "tp"),
        P(),
        P(),
        P(None, "tp"),
    )
    out_specs = (P("req", "tp"), P(None, "req", None, "tp"))
    return jax.shard_map(
        on_device, mesh=mesh, in_specs=in_specs, out_specs=out_specs, check_vma=False
    )
```

```python
import functools

import jax
import jax.numpy as jnp
import numpy as np
from jax import lax
from jax.experimental import pallas as pl
from jax.experimental.pallas import tpu as pltpu
from jax.sharding import PartitionSpec as P

EPS = 1e-06
THETA = 1000000.0


def rms_rows(values, scale_gain):
    inv_rms = lax.rsqrt(jnp.mean(values * values, axis=-1, keepdims=True) + EPS)
    return values * inv_rms * scale_gain


def rotate(values, positions):
    features = values.shape[-1]
    half_width = features // 2
    frequency = THETA ** (-(jnp.arange(half_width).astype(jnp.float32) * 2.0) / features)
    angles = positions.astype(jnp.float32)[:, None] * frequency[None, :]
    cosine = jnp.cos(angles)[:, None, :]
    sine_part = jnp.sin(angles)[:, None, :]
    first_half = values[..., :half_width]
    second_half = values[..., half_width:]
    return jnp.concatenate(
        [
            first_half * cosine - second_half * sine_part,
            second_half * cosine + first_half * sine_part,
        ],
        axis=-1,
    )


def project(normed, w_query, w_key, w_value, query_gain, key_gain, positions):
    head_dim = query_gain.shape[0]
    row_count = normed.shape[0]
    query_rows = jnp.dot(normed, w_query, preferred_element_type=jnp.float32).reshape(
        row_count, -1, head_dim
    )
    key_rows = jnp.dot(normed, w_key, preferred_element_type=jnp.float32).reshape(
        row_count, -1, head_dim
    )
    value_rows = jnp.dot(normed, w_value, preferred_element_type=jnp.float32).astype(jnp.bfloat16)
    query_rows = rotate(rms_rows(query_rows, query_gain.astype(jnp.float32)), positions).astype(
        jnp.bfloat16
    )
    key_rows = rotate(rms_rows(key_rows, key_gain.astype(jnp.float32)), positions).astype(
        jnp.bfloat16
    )
    return (query_rows.reshape(row_count, -1), key_rows.reshape(row_count, -1), value_rows)


def attend(query_slot, key_slot, value_slot, prompt_length, head_dim):
    slot_len, query_width = query_slot.shape
    kv_heads = key_slot.shape[1] // head_dim
    group_size = query_width // head_dim // kv_heads
    queries = query_slot.reshape(slot_len, kv_heads, group_size, head_dim)
    keys_split = key_slot.reshape(slot_len, kv_heads, head_dim)
    values_split = value_slot.reshape(slot_len, kv_heads, head_dim)
    scores = jnp.einsum(
        "qkgd,skd->kgqs", queries, keys_split, preferred_element_type=jnp.float32
    ) * head_dim ** (-0.5)
    offsets = jnp.arange(slot_len, dtype=jnp.int32)
    allowed = (offsets[None, :] <= offsets[:, None]) & (offsets[None, :] < prompt_length)
    scores = jnp.where(allowed[None, None], scores, -jnp.inf)
    row_max = jnp.max(scores, axis=-1, keepdims=True)
    weights = jnp.exp(scores - row_max)
    weights = (weights / jnp.sum(weights, axis=-1, keepdims=True)).astype(jnp.bfloat16)
    mixture = jnp.einsum(
        "kgqs,skd->qkgd", weights, values_split, preferred_element_type=jnp.float32
    )
    return mixture.astype(jnp.bfloat16).reshape(slot_len, query_width)


def on_device_ops(
    hidden, lengths, dealing, norm_gain, w_query, w_key, w_value, query_gain, key_gain, w_out
):
    devices = lax.axis_size("req")
    home_index = lax.axis_index("req")
    slice_index = lax.axis_index("tp")
    tok_rows, features = hidden.shape
    head_dim = query_gain.shape[0]
    out_width = w_out.shape[1]
    slot_len = 4 * tok_rows
    capacity = slot_len // devices
    prompt_total = lengths.shape[0]
    prompt_ids = jnp.arange(prompt_total, dtype=jnp.int32)
    prompt_ends = jnp.sum(
        jnp.where(prompt_ids[:, None] <= prompt_ids[None, :], lengths[:, None], 0), axis=0
    )
    starts = prompt_ends - lengths
    packed_ids = jnp.arange(tok_rows, dtype=jnp.int32) * devices + home_index
    segment = jnp.sum((packed_ids[:, None] >= prompt_ends[None, :]).astype(jnp.int32), axis=1)
    seg_onehot = (segment[:, None] == prompt_ids[None, :]).astype(jnp.int32)
    positions = packed_ids - jnp.sum(seg_onehot * starts[None, :], axis=1)
    inverse = jnp.zeros((prompt_total,), jnp.int32).at[dealing].set(prompt_ids)
    deal_hot = (dealing[:, None] == prompt_ids[None, :]).astype(jnp.int32)
    dealt_starts = jnp.sum(deal_hot * starts[None, :], axis=1)
    dealt_lengths = jnp.sum(deal_hot * lengths[None, :], axis=1)
    first_offset = jnp.mod(home_index - dealt_starts, devices)
    ranks = jnp.arange(capacity, dtype=jnp.int32)
    slot_offset = first_offset[None, :] + ranks[:, None] * devices
    send_valid = slot_offset < dealt_lengths[None, :]
    send_rows = jnp.where(
        send_valid, (dealt_starts[None, :] + slot_offset - home_index) // devices, 0
    ).reshape(-1)
    my_start = lax.dynamic_index_in_dim(dealt_starts, home_index, 0, keepdims=False)
    my_length = lax.dynamic_index_in_dim(dealt_lengths, home_index, 0, keepdims=False)
    roll_shift = jnp.mod(my_start, devices)
    my_slots = jnp.sum(seg_onehot * inverse[None, :], axis=1)
    back_rows = positions // devices * devices + my_slots
    offsets = jnp.arange(slot_len, dtype=jnp.int32)
    gain_values = norm_gain.astype(jnp.float32)
    picked = jnp.take(hidden, send_rows, axis=0).reshape(capacity, devices, hidden.shape[1])
    arrived = lax.all_to_all(
        jnp.where(send_valid[:, :, None], picked, jnp.zeros((), hidden.dtype)),
        "req",
        split_axis=1,
        concat_axis=1,
        tiled=True,
    )
    slot_hidden = jnp.roll(arrived, -roll_shift, axis=1).reshape(slot_len, arrived.shape[2])
    normed = rms_rows(slot_hidden.astype(jnp.float32), gain_values).astype(jnp.bfloat16)
    query_slot, key_slot, value_slot = project(
        normed, w_query, w_key, w_value, query_gain, key_gain, offsets
    )
    mixture = attend(query_slot, key_slot, value_slot, my_length, head_dim)
    sendback = jnp.roll(mixture.reshape(capacity, devices, mixture.shape[1]), roll_shift, axis=1)
    returned = lax.all_to_all(sendback, "req", split_axis=1, concat_axis=1, tiled=True)
    attended = jnp.take(returned.reshape(capacity * devices, -1), back_rows, axis=0)
    kv_cache = jnp.stack([key_slot, value_slot])[:, None]
    summed = jnp.dot(
        lax.all_gather(attended, "tp", axis=1, tiled=True),
        w_out,
        preferred_element_type=jnp.float32,
    )
    branch = lax.optimization_barrier(summed.astype(jnp.bfloat16))
    residual = lax.dynamic_slice_in_dim(hidden, slice_index * out_width, out_width, 1)
    hidden_out = (residual.astype(jnp.float32) + branch.astype(jnp.float32)).astype(jnp.bfloat16)
    return (hidden_out, kv_cache)


STAGES = 4
PIECES = 4
F32 = jnp.float32
BF16 = jnp.bfloat16
MESH = pl.DeviceIdType.MESH


def flip(index, mask):
    flipped = index
    bit = 1
    while bit <= mask:
        if mask & bit:
            flipped = flipped + bit * (1 - 2 * ((index // bit) % 2))
        bit *= 2
    return flipped


def pick(which, choices):
    total = jnp.zeros_like(which)
    for place, choice in enumerate(choices):
        total = total + jnp.where(which == place, choice, 0)
    return total


def whole_kernel(
    n, len_ref, deal_ref, hid_ref, gain_ref, qg_ref, kg_ref, table_ref,
    wq_hbm, wk_hbm, wv_hbm, wo_hbm, out_ref, kv_ref,
    wq, wk, wv, wo, kvb, scores, picked, att,
    w_sem, m_send, m_recv, a_send, a_recv,
):
    me = lax.axis_index("req")
    t = lax.axis_index("tp")
    yp = flip(t, 2)
    sib = flip(t, 1)
    tok = hid_ref.shape[0]
    width = wq.shape[1]
    kv_width = wk.shape[1]
    head = qg_ref.shape[1]
    kv_heads = kv_width // head
    group = width // head // kv_heads
    out_width = out_ref.shape[1]
    parts = att.shape[0]
    piece = group * head
    half = tok // PIECES
    slot_len = table_ref.shape[0]
    run = picked.shape[2]
    block = n * run

    weight_copies = [
        pltpu.make_async_copy(source, target, w_sem.at[k])
        for k, (source, target) in enumerate(
            ((wk_hbm, wk), (wv_hbm, wv), (wq_hbm, wq), (wo_hbm, wo))
        )
    ]
    for copy in weight_copies:
        copy.start()

    barrier = pltpu.get_barrier_semaphore()
    far = (4, 6, 2)
    for o in (1,) + far:
        pl.semaphore_signal(barrier, inc=1, device_id={"req": flip(me, o)}, device_id_type=MESH)
    for peer in (yp, sib):
        pl.semaphore_signal(barrier, inc=1, device_id={"tp": peer}, device_id_type=MESH)

    prompts = len_ref.shape[0]
    lens = [len_ref[p] for p in range(prompts)]
    starts = [jnp.int32(0)]
    for p in range(prompts - 1):
        starts.append(starts[-1] + lens[p])
    mine = pick(me, [deal_ref[j] for j in range(n)])
    my_start = pick(mine, starts)
    my_len = pick(mine, lens)

    row = lax.broadcasted_iota(jnp.int32, (1, tok), 1)
    col = lax.broadcasted_iota(jnp.int32, (tok, 1), 0)
    token = col * n + me
    token_start = jnp.zeros_like(token)
    for start in starts[1:]:
        token_start = jnp.maximum(token_start, jnp.where(token >= start, start, 0))

    slots = lax.broadcasted_iota(jnp.int32, (1, slot_len), 1)
    at_position = jnp.where(token - token_start == slots, 1.0, 0.0).astype(BF16)
    terms = jnp.dot(at_position, table_ref[...], preferred_element_type=F32)
    turns = terms[:, : 2 * head] + terms[:, 2 * head : 4 * head] + terms[:, 4 * head :]
    cosines, sines = turns[:, :head], turns[:, head:]

    hid = hid_ref[...].astype(F32)
    inv = lax.rsqrt(jnp.mean(hid * hid, axis=-1, keepdims=True) + EPS)
    normed = (hid * inv * gain_ref[...].astype(F32)).astype(BF16)

    def turn(values, gain):
        scaled = values * lax.rsqrt(jnp.mean(values * values, axis=-1, keepdims=True) + EPS)
        scaled = scaled * gain
        return (scaled * cosines + pltpu.roll(scaled, head // 2, 1) * sines).astype(BF16)

    def move(o, h, onward):
        source = flip(me, o) if onward else me
        rows = pl.ds(h * half, half)
        slot = o + 1 if onward else o
        return pltpu.make_async_remote_copy(
            src_ref=kvb.at[source, rows], dst_ref=kvb.at[source, rows],
            send_sem=m_send.at[slot, h], recv_sem=m_recv.at[slot, h],
            device_id={"req": flip(me, 1 if onward else o)}, device_id_type=MESH,
        )

    def share(k, g):
        which = yp if k == 2 else t
        return pltpu.make_async_remote_copy(
            src_ref=att.at[which, g], dst_ref=att.at[which, g],
            send_sem=a_send.at[k, g], recv_sem=a_recv.at[k, g],
            device_id={"tp": yp if k == 0 else sib}, device_id_type=MESH,
        )

    weight_copies[0].wait()
    weight_copies[1].wait()
    key = jnp.dot(normed, wk[...], preferred_element_type=F32)
    value = jnp.dot(normed, wv[...], preferred_element_type=F32)
    key_gain = kg_ref[...].astype(F32)
    for g in range(kv_heads):
        lanes = slice(g * head, (g + 1) * head)
        kvb[me, :, lanes] = turn(key[:, lanes], key_gain)
    kvb[me, :, kv_width:] = value.astype(BF16)
    pl.semaphore_wait(barrier, 6)
    for h in range(PIECES):
        for o in far:
            move(o, h, False).start()
        move(0, h, True).start()

    weight_copies[2].wait()
    query = jnp.dot(normed, wq[...], preferred_element_type=F32)
    query_gain = qg_ref[...].astype(F32)
    queries = [
        turn(query[:, h * head : (h + 1) * head], query_gain) for h in range(width // head)
    ]

    def onward(o, h):
        move(o, h, False).wait_recv()
        move(o, h, True).start()

    def wait_for(o):
        for h in range(PIECES):
            move(o - 1, h, True).wait_recv()

    def meet(o):
        source = flip(me, o)
        key_token = row * n + source
        allowed = (key_token <= token) & (key_token >= token_start)
        for h in range(width // head):
            g = h // group
            product = lax.dot_general(
                queries[h], kvb[source, :, g * head : (g + 1) * head],
                (((1,), (1,)), ((), ())), preferred_element_type=F32,
            )
            scores[h, :, o * tok : (o + 1) * tok] = jnp.where(
                allowed, product * head ** (-0.5), -jnp.inf
            )
        first = lax.rem(source - my_start + n * tok, n)
        begin = lax.div(my_start + first - source, n)
        step = lax.broadcasted_iota(jnp.int32, (slot_len // n, 1), 0)
        select = (row == begin + step) & (first + n * step < my_len)
        rows = jnp.dot(
            jnp.where(select, 1.0, 0.0).astype(BF16), kvb[source], preferred_element_type=F32
        ).astype(BF16)
        for i in range(STAGES):
            picked[i, source] = rows[i * run : (i + 1) * run]

    for h in range(PIECES):
        onward(2, h)
    meet(0)
    for h in range(PIECES):
        onward(4, h)
        onward(6, h)
        if h == 0:
            wait_for(1)
            meet(1)
        if h == 1:
            meet(2)
    meet(4)
    meet(6)
    for o in (3, 5, 7):
        wait_for(o)
        meet(o)

    for g in range(kv_heads):
        for k in range(group):
            h = g * group + k
            whole = scores[h]
            weights = jnp.exp(whole - jnp.max(whole, axis=-1, keepdims=True))
            weights = weights * (1.0 / jnp.sum(weights, axis=-1, keepdims=True))
            weights = weights.astype(BF16)
            lanes = slice(kv_width + g * head, kv_width + (g + 1) * head)
            mixed = jnp.zeros((tok, head), F32)
            for o in range(n):
                mixed += jnp.dot(
                    weights[:, o * tok : (o + 1) * tok], kvb[flip(me, o), :, lanes],
                    preferred_element_type=F32,
                )
            att[t, g, :, k * head : (k + 1) * head] = mixed.astype(BF16)
        share(0, g).start()
        share(1, g).start()

    share(0, 0).wait_recv()
    share(2, 0).start()

    place = n * (row % run) + lax.rem(row // run - my_start + n * tok, n)
    to_slot = jnp.where(col == place, 1.0, 0.0).astype(BF16)
    for i in range(STAGES):
        rows = jnp.dot(
            to_slot, picked[i].reshape(block, 2 * kv_width), preferred_element_type=F32
        ).astype(BF16)
        kv_ref[0, 0, i * block : (i + 1) * block, :] = rows[:, :kv_width]
        kv_ref[1, 0, i * block : (i + 1) * block, :] = rows[:, kv_width:]

    share(0, 1).wait_recv()
    share(2, 1).start()
    weight_copies[3].wait()
    for g in range(kv_heads):
        share(1, g).wait_recv()
        share(2, g).wait_recv()
    summed = jnp.zeros((tok, out_width), F32)
    for q in range(parts):
        for g in range(kv_heads):
            begin = q * width + g * piece
            summed += jnp.dot(att[q, g], wo[begin : begin + piece, :], preferred_element_type=F32)
    own = pl.ds(pl.multiple_of(t * out_width, out_width), out_width)
    branch = summed.astype(BF16).astype(F32)
    out_ref[...] = (hid_ref[:, own].astype(F32) + branch).astype(BF16)

    for h in range(PIECES):
        for o in far:
            move(o, h, False).wait_send()
        for o in (0, 2, 4, 6):
            move(o, h, True).wait_send()
    for g in range(kv_heads):
        for k in range(3):
            share(k, g).wait_send()


def on_device(
    hidden, lengths, dealing, norm_gain, w_query, w_key, w_value, query_gain, key_gain, w_out
):
    n = lax.axis_size("req")
    parts = lax.axis_size("tp")
    tok, features = hidden.shape
    head = query_gain.shape[0]
    width = w_query.shape[1]
    kv_width = w_key.shape[1]
    out_width = w_out.shape[1]
    slot_len = 4 * tok
    run = slot_len // n // STAGES
    if n != 8 or parts != 4 or run % 16 or n * run != tok:
        return on_device_ops(
            hidden, lengths, dealing, norm_gain, w_query, w_key, w_value, query_gain, key_gain, w_out
        )
    half = head // 2
    frequency = (THETA ** (-(np.arange(half) * 2.0) / head)).astype(np.float32)
    angles = np.arange(slot_len, dtype=np.float32)[:, None] * frequency[None, :]
    cosine = np.cos(angles.astype(np.float64)).astype(np.float32)
    sine = np.sin(angles.astype(np.float64)).astype(np.float32)
    exact = np.concatenate([cosine, cosine, -sine, sine], axis=1)
    terms = []
    for _ in range(3):
        terms.append(exact.astype(jnp.bfloat16))
        exact = exact - terms[-1].astype(np.float32)
    table = jnp.asarray(np.concatenate(terms, axis=1))
    smem = pl.BlockSpec(memory_space=pltpu.SMEM)
    vmem = pl.BlockSpec(memory_space=pltpu.VMEM)
    hbm = pl.BlockSpec(memory_space=pl.ANY)
    dma = pltpu.SemaphoreType.DMA
    hidden_out, kv_cache = pl.pallas_call(
        functools.partial(whole_kernel, n),
        out_shape=(
            jax.ShapeDtypeStruct((tok, out_width), BF16),
            jax.ShapeDtypeStruct((2, 1, slot_len, kv_width), BF16),
        ),
        in_specs=[smem] * 2 + [vmem] * 5 + [hbm] * 4,
        out_specs=(vmem, vmem),
        scratch_shapes=[
            pltpu.VMEM(w_query.shape, BF16),
            pltpu.VMEM(w_key.shape, BF16),
            pltpu.VMEM(w_value.shape, BF16),
            pltpu.VMEM(w_out.shape, BF16),
            pltpu.VMEM((n, tok, 2 * kv_width), BF16),
            pltpu.VMEM((width // head, tok, n * tok), F32),
            pltpu.VMEM((STAGES, n, run, 2 * kv_width), BF16),
            pltpu.VMEM((parts, kv_width // head, tok, width * head // kv_width), BF16),
            dma((4,)),
            dma((n, PIECES)),
            dma((n, PIECES)),
            dma((3, kv_width // head)),
            dma((3, kv_width // head)),
        ],
        compiler_params=pltpu.CompilerParams(
            collective_id=0, has_side_effects=True, vmem_limit_bytes=56 * 2**20
        ),
        name="attention_half",
    )(
        lengths, dealing, hidden, norm_gain.reshape(1, -1), query_gain.reshape(1, -1),
        key_gain.reshape(1, -1), table, w_query, w_key, w_value, w_out,
    )
    return hidden_out, kv_cache


def solution(mesh):
    in_specs = (
        P("req", None),
        P(),
        P(),
        P(),
        P(None, "tp"),
        P(None, "tp"),
        P(None, "tp"),
        P(),
        P(),
        P(None, "tp"),
    )
    out_specs = (P("req", "tp"), P(None, "req", None, "tp"))
    return jax.shard_map(
        on_device, mesh=mesh, in_specs=in_specs, out_specs=out_specs, check_vma=False
    )
```

```python
import functools

import jax
import jax.numpy as jnp
import numpy as np
from jax import lax
from jax.experimental import pallas as pl
from jax.experimental.pallas import tpu as pltpu
from jax.sharding import PartitionSpec as P

EPS = 1e-06
THETA = 1000000.0


def rms_rows(values, scale_gain):
    inv_rms = lax.rsqrt(jnp.mean(values * values, axis=-1, keepdims=True) + EPS)
    return values * inv_rms * scale_gain


def rotate(values, positions):
    features = values.shape[-1]
    half_width = features // 2
    frequency = THETA ** (-(jnp.arange(half_width).astype(jnp.float32) * 2.0) / features)
    angles = positions.astype(jnp.float32)[:, None] * frequency[None, :]
    cosine = jnp.cos(angles)[:, None, :]
    sine_part = jnp.sin(angles)[:, None, :]
    first_half = values[..., :half_width]
    second_half = values[..., half_width:]
    return jnp.concatenate(
        [
            first_half * cosine - second_half * sine_part,
            second_half * cosine + first_half * sine_part,
        ],
        axis=-1,
    )


def project(normed, w_query, w_key, w_value, query_gain, key_gain, positions):
    head_dim = query_gain.shape[0]
    row_count = normed.shape[0]
    query_rows = jnp.dot(normed, w_query, preferred_element_type=jnp.float32).reshape(
        row_count, -1, head_dim
    )
    key_rows = jnp.dot(normed, w_key, preferred_element_type=jnp.float32).reshape(
        row_count, -1, head_dim
    )
    value_rows = jnp.dot(normed, w_value, preferred_element_type=jnp.float32).astype(jnp.bfloat16)
    query_rows = rotate(rms_rows(query_rows, query_gain.astype(jnp.float32)), positions).astype(
        jnp.bfloat16
    )
    key_rows = rotate(rms_rows(key_rows, key_gain.astype(jnp.float32)), positions).astype(
        jnp.bfloat16
    )
    return (query_rows.reshape(row_count, -1), key_rows.reshape(row_count, -1), value_rows)


def attend(query_slot, key_slot, value_slot, prompt_length, head_dim):
    slot_len, query_width = query_slot.shape
    kv_heads = key_slot.shape[1] // head_dim
    group_size = query_width // head_dim // kv_heads
    queries = query_slot.reshape(slot_len, kv_heads, group_size, head_dim)
    keys_split = key_slot.reshape(slot_len, kv_heads, head_dim)
    values_split = value_slot.reshape(slot_len, kv_heads, head_dim)
    scores = jnp.einsum(
        "qkgd,skd->kgqs", queries, keys_split, preferred_element_type=jnp.float32
    ) * head_dim ** (-0.5)
    offsets = jnp.arange(slot_len, dtype=jnp.int32)
    allowed = (offsets[None, :] <= offsets[:, None]) & (offsets[None, :] < prompt_length)
    scores = jnp.where(allowed[None, None], scores, -jnp.inf)
    row_max = jnp.max(scores, axis=-1, keepdims=True)
    weights = jnp.exp(scores - row_max)
    weights = (weights / jnp.sum(weights, axis=-1, keepdims=True)).astype(jnp.bfloat16)
    mixture = jnp.einsum(
        "kgqs,skd->qkgd", weights, values_split, preferred_element_type=jnp.float32
    )
    return mixture.astype(jnp.bfloat16).reshape(slot_len, query_width)


def on_device_ops(
    hidden, lengths, dealing, norm_gain, w_query, w_key, w_value, query_gain, key_gain, w_out
):
    devices = lax.axis_size("req")
    home_index = lax.axis_index("req")
    slice_index = lax.axis_index("tp")
    tok_rows, features = hidden.shape
    head_dim = query_gain.shape[0]
    out_width = w_out.shape[1]
    slot_len = 4 * tok_rows
    capacity = slot_len // devices
    prompt_total = lengths.shape[0]
    prompt_ids = jnp.arange(prompt_total, dtype=jnp.int32)
    prompt_ends = jnp.sum(
        jnp.where(prompt_ids[:, None] <= prompt_ids[None, :], lengths[:, None], 0), axis=0
    )
    starts = prompt_ends - lengths
    packed_ids = jnp.arange(tok_rows, dtype=jnp.int32) * devices + home_index
    segment = jnp.sum((packed_ids[:, None] >= prompt_ends[None, :]).astype(jnp.int32), axis=1)
    seg_onehot = (segment[:, None] == prompt_ids[None, :]).astype(jnp.int32)
    positions = packed_ids - jnp.sum(seg_onehot * starts[None, :], axis=1)
    inverse = jnp.zeros((prompt_total,), jnp.int32).at[dealing].set(prompt_ids)
    deal_hot = (dealing[:, None] == prompt_ids[None, :]).astype(jnp.int32)
    dealt_starts = jnp.sum(deal_hot * starts[None, :], axis=1)
    dealt_lengths = jnp.sum(deal_hot * lengths[None, :], axis=1)
    first_offset = jnp.mod(home_index - dealt_starts, devices)
    ranks = jnp.arange(capacity, dtype=jnp.int32)
    slot_offset = first_offset[None, :] + ranks[:, None] * devices
    send_valid = slot_offset < dealt_lengths[None, :]
    send_rows = jnp.where(
        send_valid, (dealt_starts[None, :] + slot_offset - home_index) // devices, 0
    ).reshape(-1)
    my_start = lax.dynamic_index_in_dim(dealt_starts, home_index, 0, keepdims=False)
    my_length = lax.dynamic_index_in_dim(dealt_lengths, home_index, 0, keepdims=False)
    roll_shift = jnp.mod(my_start, devices)
    my_slots = jnp.sum(seg_onehot * inverse[None, :], axis=1)
    back_rows = positions // devices * devices + my_slots
    offsets = jnp.arange(slot_len, dtype=jnp.int32)
    gain_values = norm_gain.astype(jnp.float32)
    picked = jnp.take(hidden, send_rows, axis=0).reshape(capacity, devices, hidden.shape[1])
    arrived = lax.all_to_all(
        jnp.where(send_valid[:, :, None], picked, jnp.zeros((), hidden.dtype)),
        "req",
        split_axis=1,
        concat_axis=1,
        tiled=True,
    )
    slot_hidden = jnp.roll(arrived, -roll_shift, axis=1).reshape(slot_len, arrived.shape[2])
    normed = rms_rows(slot_hidden.astype(jnp.float32), gain_values).astype(jnp.bfloat16)
    query_slot, key_slot, value_slot = project(
        normed, w_query, w_key, w_value, query_gain, key_gain, offsets
    )
    mixture = attend(query_slot, key_slot, value_slot, my_length, head_dim)
    sendback = jnp.roll(mixture.reshape(capacity, devices, mixture.shape[1]), roll_shift, axis=1)
    returned = lax.all_to_all(sendback, "req", split_axis=1, concat_axis=1, tiled=True)
    attended = jnp.take(returned.reshape(capacity * devices, -1), back_rows, axis=0)
    kv_cache = jnp.stack([key_slot, value_slot])[:, None]
    summed = jnp.dot(
        lax.all_gather(attended, "tp", axis=1, tiled=True),
        w_out,
        preferred_element_type=jnp.float32,
    )
    branch = lax.optimization_barrier(summed.astype(jnp.bfloat16))
    residual = lax.dynamic_slice_in_dim(hidden, slice_index * out_width, out_width, 1)
    hidden_out = (residual.astype(jnp.float32) + branch.astype(jnp.float32)).astype(jnp.bfloat16)
    return (hidden_out, kv_cache)


STAGES = 4
PIECES = 4
F32 = jnp.float32
BF16 = jnp.bfloat16
MESH = pl.DeviceIdType.MESH


def flip(index, mask):
    flipped = index
    bit = 1
    while bit <= mask:
        if mask & bit:
            flipped = flipped + bit * (1 - 2 * ((index // bit) % 2))
        bit *= 2
    return flipped


def pick(which, choices):
    total = jnp.zeros_like(which)
    for place, choice in enumerate(choices):
        total = total + jnp.where(which == place, choice, 0)
    return total


def whole_kernel(
    n, len_ref, deal_ref, hid_ref, gain_ref, qg_ref, kg_ref, table_ref,
    wq_hbm, wk_hbm, wv_hbm, wo_hbm, out_ref, kv_ref,
    wq, wk, wv, wo, kvb, scores, picked, att,
    w_sem, m_send, m_recv, a_send, a_recv,
):
    me = lax.axis_index("req")
    t = lax.axis_index("tp")
    yp = flip(t, 2)
    sib = flip(t, 1)
    tok = hid_ref.shape[0]
    width = wq.shape[1]
    kv_width = wk.shape[1]
    head = qg_ref.shape[1]
    kv_heads = kv_width // head
    group = width // head // kv_heads
    out_width = out_ref.shape[1]
    parts = att.shape[0]
    piece = group * head
    half = tok // PIECES
    slot_len = table_ref.shape[0]
    run = picked.shape[2]
    block = n * run

    weight_copies = [
        pltpu.make_async_copy(source, target, w_sem.at[k])
        for k, (source, target) in enumerate(
            ((wk_hbm, wk), (wv_hbm, wv), (wq_hbm, wq), (wo_hbm, wo))
        )
    ]
    for copy in weight_copies:
        copy.start()

    barrier = pltpu.get_barrier_semaphore()
    far = (4, 6, 2)
    for o in (1,) + far:
        pl.semaphore_signal(barrier, inc=1, device_id={"req": flip(me, o)}, device_id_type=MESH)
    for peer in (yp, sib):
        pl.semaphore_signal(barrier, inc=1, device_id={"tp": peer}, device_id_type=MESH)

    prompts = len_ref.shape[0]
    lens = [len_ref[p] for p in range(prompts)]
    starts = [jnp.int32(0)]
    for p in range(prompts - 1):
        starts.append(starts[-1] + lens[p])
    mine = pick(me, [deal_ref[j] for j in range(n)])
    my_start = pick(mine, starts)
    my_len = pick(mine, lens)

    row = lax.broadcasted_iota(jnp.int32, (1, tok), 1)
    col = lax.broadcasted_iota(jnp.int32, (tok, 1), 0)
    token = col * n + me
    token_start = jnp.zeros_like(token)
    for start in starts[1:]:
        token_start = jnp.maximum(token_start, jnp.where(token >= start, start, 0))

    slots = lax.broadcasted_iota(jnp.int32, (1, slot_len), 1)
    at_position = jnp.where(token - token_start == slots, 1.0, 0.0).astype(BF16)
    terms = jnp.dot(at_position, table_ref[...], preferred_element_type=F32)
    turns = terms[:, : 2 * head] + terms[:, 2 * head : 4 * head] + terms[:, 4 * head :]
    cosines, sines = turns[:, :head], turns[:, head:]

    hid = hid_ref[...].astype(F32)
    inv = lax.rsqrt(jnp.mean(hid * hid, axis=-1, keepdims=True) + EPS)
    normed = (hid * inv * gain_ref[...].astype(F32)).astype(BF16)

    def turn(values, gain):
        scaled = values * lax.rsqrt(jnp.mean(values * values, axis=-1, keepdims=True) + EPS)
        scaled = scaled * gain
        return (scaled * cosines + pltpu.roll(scaled, head // 2, 1) * sines).astype(BF16)

    def move(o, h, onward):
        source = flip(me, o) if onward else me
        rows = pl.ds(h * half, half)
        slot = o + 1 if onward else o
        return pltpu.make_async_remote_copy(
            src_ref=kvb.at[source, rows], dst_ref=kvb.at[source, rows],
            send_sem=m_send.at[slot, h], recv_sem=m_recv.at[slot, h],
            device_id={"req": flip(me, 1 if onward else o)}, device_id_type=MESH,
        )

    def share(k, g):
        which = yp if k == 2 else t
        return pltpu.make_async_remote_copy(
            src_ref=att.at[which, g], dst_ref=att.at[which, g],
            send_sem=a_send.at[k, g], recv_sem=a_recv.at[k, g],
            device_id={"tp": yp if k == 0 else sib}, device_id_type=MESH,
        )

    weight_copies[0].wait()
    weight_copies[1].wait()
    key = jnp.dot(normed, wk[...], preferred_element_type=F32)
    value = jnp.dot(normed, wv[...], preferred_element_type=F32)
    key_gain = kg_ref[...].astype(F32)
    for g in range(kv_heads):
        lanes = slice(g * head, (g + 1) * head)
        kvb[me, :, lanes] = turn(key[:, lanes], key_gain)
    kvb[me, :, kv_width:] = value.astype(BF16)
    pl.semaphore_wait(barrier, 6)
    for h in range(PIECES):
        for o in far:
            move(o, h, False).start()
        move(0, h, True).start()

    weight_copies[2].wait()
    query = jnp.dot(normed, wq[...], preferred_element_type=F32)
    query_gain = qg_ref[...].astype(F32)
    queries = [
        turn(query[:, h * head : (h + 1) * head], query_gain) for h in range(width // head)
    ]

    tops = [jnp.full((tok, 1), -jnp.inf, F32)] * len(queries)

    def onward(o, h):
        move(o, h, False).wait_recv()
        move(o, h, True).start()

    def wait_for(o):
        for h in range(PIECES):
            move(o - 1, h, True).wait_recv()

    def meet(o):
        source = flip(me, o)
        key_token = row * n + source
        allowed = (key_token <= token) & (key_token >= token_start)
        for h in range(width // head):
            g = h // group
            product = lax.dot_general(
                queries[h], kvb[source, :, g * head : (g + 1) * head],
                (((1,), (1,)), ((), ())), preferred_element_type=F32,
            )
            tile = jnp.where(allowed, product * head ** (-0.5), -jnp.inf)
            scores[h, :, o * tok : (o + 1) * tok] = tile
            tops[h] = jnp.maximum(tops[h], jnp.max(tile, axis=-1, keepdims=True))
        first = lax.rem(source - my_start + n * tok, n)
        begin = lax.div(my_start + first - source, n)
        step = lax.broadcasted_iota(jnp.int32, (slot_len // n, 1), 0)
        select = (row == begin + step) & (first + n * step < my_len)
        rows = jnp.dot(
            jnp.where(select, 1.0, 0.0).astype(BF16), kvb[source], preferred_element_type=F32
        ).astype(BF16)
        for i in range(STAGES):
            picked[i, source] = rows[i * run : (i + 1) * run]

    for h in range(PIECES):
        onward(2, h)
    meet(0)
    for h in range(PIECES):
        onward(4, h)
        onward(6, h)
        if h == 0:
            wait_for(1)
            meet(1)
        if h == 1:
            meet(2)
    meet(4)
    meet(6)
    for o in (3, 5, 7):
        wait_for(o)
        meet(o)

    for g in range(kv_heads):
        for k in range(group):
            h = g * group + k
            weights = jnp.exp(scores[h] - tops[h])
            weights = weights * (1.0 / jnp.sum(weights, axis=-1, keepdims=True))
            weights = weights.astype(BF16)
            lanes = slice(kv_width + g * head, kv_width + (g + 1) * head)
            mixed = jnp.zeros((tok, head), F32)
            for o in range(n):
                mixed += jnp.dot(
                    weights[:, o * tok : (o + 1) * tok], kvb[flip(me, o), :, lanes],
                    preferred_element_type=F32,
                )
            att[t, g, :, k * head : (k + 1) * head] = mixed.astype(BF16)
        share(0, g).start()
        share(1, g).start()

    share(0, 0).wait_recv()
    share(2, 0).start()

    place = n * (row % run) + lax.rem(row // run - my_start + n * tok, n)
    to_slot = jnp.where(col == place, 1.0, 0.0).astype(BF16)
    for i in range(STAGES):
        rows = jnp.dot(
            to_slot, picked[i].reshape(block, 2 * kv_width), preferred_element_type=F32
        ).astype(BF16)
        kv_ref[0, 0, i * block : (i + 1) * block, :] = rows[:, :kv_width]
        kv_ref[1, 0, i * block : (i + 1) * block, :] = rows[:, kv_width:]

    share(0, 1).wait_recv()
    share(2, 1).start()
    weight_copies[3].wait()
    for g in range(kv_heads):
        share(1, g).wait_recv()
        share(2, g).wait_recv()
    summed = jnp.zeros((tok, out_width), F32)
    for q in range(parts):
        for g in range(kv_heads):
            begin = q * width + g * piece
            summed += jnp.dot(att[q, g], wo[begin : begin + piece, :], preferred_element_type=F32)
    own = pl.ds(pl.multiple_of(t * out_width, out_width), out_width)
    branch = summed.astype(BF16).astype(F32)
    out_ref[...] = (hid_ref[:, own].astype(F32) + branch).astype(BF16)

    for h in range(PIECES):
        for o in far:
            move(o, h, False).wait_send()
        for o in (0, 2, 4, 6):
            move(o, h, True).wait_send()
    for g in range(kv_heads):
        for k in range(3):
            share(k, g).wait_send()


def on_device(
    hidden, lengths, dealing, norm_gain, w_query, w_key, w_value, query_gain, key_gain, w_out
):
    n = lax.axis_size("req")
    parts = lax.axis_size("tp")
    tok, features = hidden.shape
    head = query_gain.shape[0]
    width = w_query.shape[1]
    kv_width = w_key.shape[1]
    out_width = w_out.shape[1]
    slot_len = 4 * tok
    run = slot_len // n // STAGES
    if n != 8 or parts != 4 or run % 16 or n * run != tok:
        return on_device_ops(
            hidden, lengths, dealing, norm_gain, w_query, w_key, w_value, query_gain, key_gain, w_out
        )
    half = head // 2
    frequency = (THETA ** (-(np.arange(half) * 2.0) / head)).astype(np.float32)
    angles = np.arange(slot_len, dtype=np.float32)[:, None] * frequency[None, :]
    cosine = np.cos(angles.astype(np.float64)).astype(np.float32)
    sine = np.sin(angles.astype(np.float64)).astype(np.float32)
    exact = np.concatenate([cosine, cosine, -sine, sine], axis=1)
    terms = []
    for _ in range(3):
        terms.append(exact.astype(jnp.bfloat16))
        exact = exact - terms[-1].astype(np.float32)
    table = jnp.asarray(np.concatenate(terms, axis=1))
    smem = pl.BlockSpec(memory_space=pltpu.SMEM)
    vmem = pl.BlockSpec(memory_space=pltpu.VMEM)
    hbm = pl.BlockSpec(memory_space=pl.ANY)
    dma = pltpu.SemaphoreType.DMA
    hidden_out, kv_cache = pl.pallas_call(
        functools.partial(whole_kernel, n),
        out_shape=(
            jax.ShapeDtypeStruct((tok, out_width), BF16),
            jax.ShapeDtypeStruct((2, 1, slot_len, kv_width), BF16),
        ),
        in_specs=[smem] * 2 + [vmem] * 5 + [hbm] * 4,
        out_specs=(vmem, vmem),
        scratch_shapes=[
            pltpu.VMEM(w_query.shape, BF16),
            pltpu.VMEM(w_key.shape, BF16),
            pltpu.VMEM(w_value.shape, BF16),
            pltpu.VMEM(w_out.shape, BF16),
            pltpu.VMEM((n, tok, 2 * kv_width), BF16),
            pltpu.VMEM((width // head, tok, n * tok), F32),
            pltpu.VMEM((STAGES, n, run, 2 * kv_width), BF16),
            pltpu.VMEM((parts, kv_width // head, tok, width * head // kv_width), BF16),
            dma((4,)),
            dma((n, PIECES)),
            dma((n, PIECES)),
            dma((3, kv_width // head)),
            dma((3, kv_width // head)),
        ],
        compiler_params=pltpu.CompilerParams(
            collective_id=0, has_side_effects=True, vmem_limit_bytes=56 * 2**20
        ),
        name="attention_half",
    )(
        lengths, dealing, hidden, norm_gain.reshape(1, -1), query_gain.reshape(1, -1),
        key_gain.reshape(1, -1), table, w_query, w_key, w_value, w_out,
    )
    return hidden_out, kv_cache


def solution(mesh):
    in_specs = (
        P("req", None),
        P(),
        P(),
        P(),
        P(None, "tp"),
        P(None, "tp"),
        P(None, "tp"),
        P(),
        P(),
        P(None, "tp"),
    )
    out_specs = (P("req", "tp"), P(None, "req", None, "tp"))
    return jax.shard_map(
        on_device, mesh=mesh, in_specs=in_specs, out_specs=out_specs, check_vma=False
    )
```
